32 devices in a mesh: groups: 2 (over y), tensor: 4 (over z), expert: 4 (over x, core).
Axes of the slice: x: 2, y: 2, z: 4, core: 2. Of those that a mesh axis runs over, the one named last changes fastest.
Arguments:
- center: bfloat16 [32, 6144], P(('groups', 'expert')), parts along dimension 0, may hold values from -6 to 6
- gens: bfloat16 [32, 64, 6144], P(('groups', 'expert'), 'tensor'), parts along dimension 0, may hold values from -3 to 3
- query: bfloat16 [32, 6144], P(('groups', 'expert')), parts along dimension 0, may hold values from -6 to 6
- routes: int32 [32, 2], P(('groups', 'expert')), parts along dimension 0, may hold values from 0 to 3, as said below
- route_weights: float32 [32, 2], P(('groups', 'expert')), parts along dimension 0, may hold values from 0.25 to 1
- gate_weight: bfloat16 [4, 6144, 8192], P('expert', None, 'tensor'), may hold values from -0.078125 to 0.078125
- up_weight: bfloat16 [4, 6144, 8192], P('expert', None, 'tensor'), may hold values from -0.078125 to 0.078125
- down_weight: bfloat16 [4, 8192, 6144], P('expert', 'tensor'), may hold values from -0.0625 to 0.0625
- block_mask: int32 [4, 3, 48, 64], P('expert', None, None, 'tensor'), may hold values 0 or 1
Outputs:
- center_out: bfloat16 [32, 6144], P(('groups', 'expert')), parts along dimension 0
- gens_out: bfloat16 [32, 64, 6144], P(('groups', 'expert'), 'tensor'), parts along dimension 0
- radius: float32 [32, 6144], P(('groups', 'expert')), parts along dimension 0
- adjoint: float32 [32, 6144], P(('groups', 'expert')), parts along dimension 0
The draws below stay inside these ranges and needn't reach their ends.
There are 2 independent parts, one for each index of `groups`. The reference program is written for one: setup_inputs(seed, part) draws one part's arguments, and reference() takes and returns one part's arrays. A program takes and returns all parts, laid end to end along the dimension named above; an argument that names none is the same for every part. Nothing has to cross between parts.
Inputs may be any that keep to these rules, and one draw needn't show every extreme that they name: `routes`: each token names two different experts. In every aligned block of 4 tokens (those of one index of expert), no expert is named by more than 3 tokens, and one expert, the same in all blocks of a draw, is named by exactly 3.
All inputs are finite; a program needn't handle non-finite values. No bound on the sum of `block_mask` on one device may be relied on, other than what follows from the above.
Results may differ from the reference program's by a relative error of at most 0.0075.
Values may be sent and summed in bfloat16 or wider, within the bound.
A program may use at most 512 MiB of HBM per device.

```python
import math
import jax
import jax.numpy as jnp
from jax import lax

D = 6144
F = 8192
GENS = 64
BLK = 128
TOK_DEV = 4
EXPERTS = 4
MOST = 3
TOKENS = 16


def draw_routes(key, part):
    block_count = TOKENS // TOK_DEV
    key_hot, key_order, key_rotation, key_partner, key_swap = jax.random.split(key, 5)
    hot_expert = jax.random.randint(key_hot, (), 0, EXPERTS)
    other_experts = (hot_expert + 1 + jnp.arange(EXPERTS - 1, dtype=jnp.int32)) % EXPERTS
    ordering = jax.vmap(lambda k: jax.random.permutation(k, TOK_DEV))(jax.random.split(key_order, block_count))
    position = jnp.argsort(ordering, axis=1)
    rotation = jax.vmap(lambda k: jax.random.permutation(k, EXPERTS - 1))(jax.random.split(key_rotation, block_count))
    partner_draw = jax.vmap(lambda k: jax.random.permutation(k, EXPERTS - 1))(jax.random.split(key_partner, block_count * TOK_DEV))
    partner_draw = partner_draw.reshape(block_count, TOK_DEV, EXPERTS - 1)
    is_hot = position < MOST
    hot_partner = other_experts[jnp.take_along_axis(rotation, position % (EXPERTS - 1), axis=1)]
    leading = jnp.where(is_hot, hot_expert, other_experts[partner_draw[:, :, 0]])
    trailing = jnp.where(is_hot, hot_partner, other_experts[partner_draw[:, :, 1]])
    swapped = jax.random.randint(key_swap, (block_count, TOK_DEV), 0, 2)
    column_one = jnp.where(swapped == 1, trailing, leading)
    column_two = jnp.where(swapped == 1, leading, trailing)
    return jnp.stack([column_one, column_two], axis=-1).reshape(TOKENS, 2).astype(jnp.int32)


def plant(values, stream_key, low, largest):
    longest = values.shape.index(max(values.shape))
    spots = []
    for shift in (0, 1):
        where = [jax.random.randint(jax.random.fold_in(stream_key, axis), (), 0, length) for axis, length in enumerate(values.shape)]
        where[longest] = (where[longest] + shift) % values.shape[longest]
        spots.append(tuple(where))
    return values.at[spots[0]].set(low).at[spots[1]].set(largest)


def level_of(rng, dims, cuts, low, largest):
    factor_of, own = 1.0, jax.random.fold_in(rng, 6)
    for dim, parts in cuts:
        steps = jnp.exp(jax.random.uniform(jax.random.fold_in(own, dim), (parts,), jnp.float32, low / len(cuts), largest / len(cuts)))
        factor_of = factor_of * jnp.repeat(steps, dims[dim] // parts).reshape([-1 if axis == dim else 1 for axis in range(len(dims))])
    return factor_of


def centred(stream_key, extent, scale, most, pieces=(), kind=jnp.bfloat16):
    loudness = level_of(stream_key, extent, pieces, -0.22, 0.18) if pieces else 1.0
    result = jax.random.normal(stream_key, extent, jnp.float32) * scale * loudness
    return jnp.minimum(jnp.maximum(result, -most), most).astype(kind)


def setup_inputs(seed: int = 0, part: int = 0) -> dict:
    seeds = jax.random.split(jax.random.key(seed), 10)
    part_splits = jax.random.split(jax.random.fold_in(seeds[9], part), 10)
    center = centred(part_splits[0], (TOKENS, D), 1.0, 6.0, ((0, 4),))
    gens = centred(part_splits[1], (TOKENS, GENS, D), 0.5, 3.0, ((0, 4), (1, 4)))
    query = centred(part_splits[2], (TOKENS, D), 1.0, 6.0, ((0, 4),))
    routes = draw_routes(jax.random.fold_in(jax.random.fold_in(seeds[9], part), 71), part)
    route_weights = jnp.clip(jnp.exp(math.log(1.0) - 1.3862944 * jax.random.uniform(part_splits[4], (TOKENS, 2), jnp.float32) ** level_of(part_splits[4], (TOKENS, 2), ((0, 4),), -0.2, 0.2)), 0.25, 1.0)
    gate_weight = centred(seeds[5], (EXPERTS, D, F), D ** -0.5, 0.078125, ((0, 4), (2, 4)))
    up_weight = centred(seeds[6], (EXPERTS, D, F), D ** -0.5, 0.078125, ((0, 4), (2, 4)))
    down_weight = centred(seeds[7], (EXPERTS, F, D), F ** -0.5, 0.0625, ((0, 4), (1, 4)))
    block_mask = plant((jax.random.randint(seeds[8], (EXPERTS, 3, D // BLK, F // BLK), 0, 10) < 7).astype(jnp.int32), jax.random.fold_in(seeds[8], 1), 0, 1)
    return {"center": center, "gens": gens, "query": query, "routes": routes, "route_weights": route_weights, "gate_weight": gate_weight, "up_weight": up_weight, "down_weight": down_weight, "block_mask": block_mask}


def reference(center, gens, query, routes, route_weights, gate_weight, up_weight, down_weight, block_mask):
    nd = D // BLK
    nf = F // BLK
    mask_all = block_mask.astype(gate_weight.dtype)
    gate_all = (gate_weight.reshape(EXPERTS, nd, BLK, nf, BLK) * mask_all[:, 0][:, :, None, :, None]).reshape(EXPERTS, D, F)
    up_all = (up_weight.reshape(EXPERTS, nd, BLK, nf, BLK) * mask_all[:, 1][:, :, None, :, None]).reshape(EXPERTS, D, F)
    down_mask = jnp.transpose(mask_all[:, 2], (0, 2, 1))
    down_all = (down_weight.reshape(EXPERTS, nf, BLK, nd, BLK) * down_mask[:, :, None, :, None]).reshape(EXPERTS, F, D)
    flat_ids = jnp.arange(TOKENS * 2, dtype=jnp.int32)

    def one_route(index):
        token = index // 2
        column = index % 2
        expert = routes[token, column]
        w_gate = gate_all[expert]
        w_up = up_all[expert]
        w_down = down_all[expert]
        center_row = center[token][None]
        gen_rows = gens[token]
        query_row = query[token][None]
        gate_center = jnp.dot(center_row, w_gate, preferred_element_type=jnp.float32)[0]
        up_center = jnp.dot(center_row, w_up, preferred_element_type=jnp.float32)[0]
        gate_gens = jnp.dot(gen_rows, w_gate, preferred_element_type=jnp.float32)
        up_gens = jnp.dot(gen_rows, w_up, preferred_element_type=jnp.float32)
        sigma = 1.0 / (1.0 + jnp.exp(-gate_center))
        activated = gate_center * sigma
        slope_gate = sigma * (1.0 + gate_center * (1.0 - sigma)) * up_center
        hidden_center = (activated * up_center).astype(jnp.bfloat16)
        hidden_gens = (slope_gate[None] * gate_gens + activated[None] * up_gens).astype(jnp.bfloat16)
        out_center = jnp.dot(hidden_center[None], w_down, preferred_element_type=jnp.float32)[0]
        out_gens = jnp.dot(hidden_gens, w_down, preferred_element_type=jnp.float32)
        adjoint_hidden = jnp.dot(query_row, w_down.T, preferred_element_type=jnp.float32)[0]
        adjoint_gate = (adjoint_hidden * slope_gate).astype(jnp.bfloat16)
        adjoint_up = (adjoint_hidden * activated).astype(jnp.bfloat16)
        adjoint_in = jnp.dot(adjoint_gate[None], w_gate.T, preferred_element_type=jnp.float32)[0]
        adjoint_in = adjoint_in + jnp.dot(adjoint_up[None], w_up.T, preferred_element_type=jnp.float32)[0]
        return out_center, out_gens, adjoint_in

    out_center, out_gens, adjoint_in = lax.map(one_route, flat_ids)
    weights = route_weights.reshape(TOKENS * 2)
    token_center = (out_center * weights[:, None]).reshape(TOKENS, 2, D).sum(axis=1)
    token_gens = (out_gens * weights[:, None, None]).reshape(TOKENS, 2, GENS, D).sum(axis=1)
    adjoint = (adjoint_in * weights[:, None]).reshape(TOKENS, 2, D).sum(axis=1)
    radius = jnp.sum(jnp.abs(token_gens), axis=1)
    return (token_center.astype(jnp.bfloat16), token_gens.astype(jnp.bfloat16), radius, adjoint)
```

```python
import functools

import jax
import jax.numpy as jnp
from jax import lax
from jax.experimental import pallas as pl
from jax.experimental.pallas import tpu as pltpu
from jax.sharding import PartitionSpec as P

BLK = 128
MOST = 3
CHUNKS_IN = 3
CHUNKS_OUT = 4
COST_SHARE = 20
VMEM = 56 * 2**20
F32 = jnp.float32
BF16 = jnp.bfloat16


def params():
    return pltpu.CompilerParams(vmem_limit_bytes=VMEM)


def cost(flops, nbytes):
    return pl.CostEstimate(
        flops=flops // COST_SHARE, bytes_accessed=nbytes // COST_SHARE, transcendentals=0
    )


def after(value, *others):
    return lax.optimization_barrier((value, *others))[0]


def mask_in_kernel(gate_ref, up_ref, gate_mask, up_mask, center_ref, *refs):
    gate_out, up_out, gc_ref, uc_ref = refs[-4:]
    for k in range(gate_ref.shape[0] // BLK):
        rows = slice(k * BLK, (k + 1) * BLK)
        gate_out[rows, :] = gate_ref[rows, :] * gate_mask[k : k + 1, :]
        up_out[rows, :] = up_ref[rows, :] * up_mask[k : k + 1, :]
    center = center_ref[...]
    gc_ref[...] = jnp.dot(center, gate_out[...], preferred_element_type=F32)
    uc_ref[...] = jnp.dot(center, up_out[...], preferred_element_type=F32)


def mask_in(gate, up, gate_mask, up_mask, center, part, parts, before):
    width, hidden = gate.shape
    tokens = center.shape[0]
    tile = min(256, hidden // parts)
    steps = hidden // parts // tile
    start = part * steps
    weight = pl.BlockSpec((width, tile), lambda n: (0, start + n))
    mask = pl.BlockSpec((width // BLK, tile), lambda n: (0, start + n))
    pre = pl.BlockSpec((tokens, tile), lambda n: (0, n))
    return pl.pallas_call(
        mask_in_kernel,
        grid=(steps,),
        in_specs=[weight, weight, mask, mask, pl.BlockSpec((tokens, width), lambda n: (0, 0))]
        + [pl.BlockSpec(memory_space=pl.ANY)] * len(before),
        out_specs=[weight, weight, pre, pre],
        out_shape=[
            jax.ShapeDtypeStruct((width, hidden), BF16),
            jax.ShapeDtypeStruct((width, hidden), BF16),
            jax.ShapeDtypeStruct((tokens, hidden // parts), F32),
            jax.ShapeDtypeStruct((tokens, hidden // parts), F32),
        ],
        input_output_aliases={5 + i: i for i in range(len(before))},
        compiler_params=params(),
        cost_estimate=cost(4 * tokens * width * hidden // parts, 8 * width * hidden // parts),
        name="mask_in",
    )(gate, up, gate_mask, up_mask, center, *before)


def mask_down_kernel(down_ref, mask_ref, query_ref, down_out, lam_ref):
    for k in range(down_ref.shape[0] // BLK):
        rows = slice(k * BLK, (k + 1) * BLK)
        down_out[rows, :] = down_ref[rows, :] * mask_ref[k : k + 1, :]

    @pl.when(pl.program_id(0) == 0)
    def _():
        lam_ref[...] = jnp.zeros_like(lam_ref)

    lam_ref[...] += lax.dot_general(
        query_ref[...], down_out[...], (((1,), (1,)), ((), ())), preferred_element_type=F32
    )


def mask_down(down, mask, query):
    hidden, width = down.shape
    tokens = query.shape[0]
    tile = 512
    return pl.pallas_call(
        mask_down_kernel,
        grid=(width // tile,),
        in_specs=[
            pl.BlockSpec((hidden, tile), lambda n: (0, n)),
            pl.BlockSpec((hidden // BLK, tile), lambda n: (0, n)),
            pl.BlockSpec((tokens, tile), lambda n: (0, n)),
        ],
        out_specs=[
            pl.BlockSpec((hidden, tile), lambda n: (0, n)),
            pl.BlockSpec((tokens, hidden), lambda n: (0, 0)),
        ],
        out_shape=[
            jax.ShapeDtypeStruct((hidden, width), BF16),
            jax.ShapeDtypeStruct((tokens, hidden), F32),
        ],
        compiler_params=params(),
        cost_estimate=cost(2 * tokens * width * hidden, 4 * width * hidden),
        name="mask_down",
    )(down, mask, query)


def gens_in_kernel(chunks, tok_ref, *refs):
    sides = (len(refs) - 6) // chunks
    parts = refs[: sides * chunks]
    gate_ref, up_ref, slope_ref, act_ref, out_ref, rows_ref = refs[sides * chunks :]
    lead, tokens, group, cols = parts[0].shape
    all_rows = lead * group
    slots = sides * MOST

    @pl.when(pl.program_id(0) == 0)
    def _():
        for s in range(slots):
            side = s // MOST
            tok = tok_ref[s]
            for c in range(chunks):
                for z in range(lead):
                    at = s * all_rows + z * group
                    rows_ref[at : at + group, c * cols : (c + 1) * cols] = parts[
                        side * chunks + c
                    ][z, tok]

    gate = jnp.dot(rows_ref[...], gate_ref[...], preferred_element_type=F32)
    up = jnp.dot(rows_ref[...], up_ref[...], preferred_element_type=F32)
    for s in range(slots):
        tok = tok_ref[s] + tokens * (s // MOST)
        here = slice(s * all_rows, (s + 1) * all_rows)
        out_ref[here, :] = (
            slope_ref[tok] * gate[here, :] + act_ref[tok] * up[here, :]
        ).astype(BF16)


def gens_in(tok, blocks, gate, up, slope, act):
    width, hidden = gate.shape
    chunks = len(blocks[0])
    sides = len(blocks)
    lead, tokens, group, _ = blocks[0][0].shape
    rows = sides * MOST * lead * group
    tile = min(256, hidden)
    part = pl.BlockSpec(
        blocks[0][0].shape, lambda n, t: (0, 0, 0, 0), pipeline_mode=pl.Buffered(1)
    )
    weight = pl.BlockSpec((width, tile), lambda n, t: (0, n))
    coef = pl.BlockSpec((sides * tokens, 1, tile), lambda n, t: (0, 0, n))
    return pl.pallas_call(
        functools.partial(gens_in_kernel, chunks),
        grid_spec=pltpu.PrefetchScalarGridSpec(
            num_scalar_prefetch=1,
            grid=(hidden // tile,),
            in_specs=[part] * (sides * chunks) + [weight, weight, coef, coef],
            out_specs=pl.BlockSpec((rows, tile), lambda n, t: (0, n)),
            scratch_shapes=[pltpu.VMEM((rows, width), BF16)],
        ),
        out_shape=jax.ShapeDtypeStruct((rows, hidden), BF16),
        compiler_params=params(),
        cost_estimate=cost(4 * rows * width * hidden, 4 * width * hidden + 2 * rows * width),
        name="gens_in",
    )(tok, *[p for block in blocks for p in block], gate, up, slope, act)


def gens_out_kernel(tok_ref, valid_ref, weight_ref, hidden_ref, down_ref, *out_refs):
    lead, _, group, _ = out_refs[0].shape
    all_rows = lead * group
    for out_ref in out_refs:
        out_ref[...] = jnp.zeros_like(out_ref)
    total = jnp.dot(hidden_ref[...], down_ref[...], preferred_element_type=F32)
    for s in range(len(out_refs) * MOST):
        out_ref = out_refs[s // MOST]

        @pl.when(valid_ref[s] > 0)
        def _():
            for z in range(lead):
                at = s * all_rows + z * group
                out_ref[z, tok_ref[s]] = (total[at : at + group, :] * weight_ref[s]).astype(BF16)


def gens_out(tok, valid, weight, hidden_gens, down, chunk, cols, lead, tokens, sides):
    rows, hidden = hidden_gens.shape
    group = rows // (sides * MOST * lead)
    tile = 512
    start = chunk * cols // tile
    return pl.pallas_call(
        gens_out_kernel,
        grid_spec=pltpu.PrefetchScalarGridSpec(
            num_scalar_prefetch=3,
            grid=(cols // tile,),
            in_specs=[
                pl.BlockSpec((rows, hidden), lambda n, *_: (0, 0), pipeline_mode=pl.Buffered(1)),
                pl.BlockSpec((hidden, tile), lambda n, *_: (0, start + n)),
            ],
            out_specs=[
                pl.BlockSpec((lead, tokens, group, tile), lambda n, *_: (0, 0, 0, n))
            ]
            * sides,
        ),
        out_shape=[jax.ShapeDtypeStruct((lead, tokens, group, cols), BF16)] * sides,
        compiler_params=params(),
        cost_estimate=cost(2 * rows * hidden * cols, 2 * hidden * cols + 4 * rows * cols),
        name="gens_out",
    )(tok, valid, weight, hidden_gens, down)


def shards(
    center, gens, query, routes, route_weights, gate_weight, up_weight, down_weight, block_mask
):
    experts = lax.axis_size("expert")
    tensors = lax.axis_size("tensor")
    tokens, rows_here, width = gens.shape
    me = lax.axis_index("expert")

    def across(value, distance):
        return lax.ppermute(value, "expert", [(i, i ^ distance) for i in range(experts)])

    pair = jnp.concatenate([center, query], axis=0)
    info = jnp.concatenate([routes.astype(F32), route_weights], axis=1)
    pairs = [pair] + [across(pair, r) for r in range(1, experts)]
    infos = jnp.stack([info] + [across(info, r) for r in range(1, experts)])
    center_all = jnp.concatenate([p[:tokens] for p in pairs], axis=0)
    query_all = jnp.concatenate([p[tokens:] for p in pairs], axis=0)

    aligned = rows_here % 16 == 0

    def back(value, distance):
        return lax.ppermute(
            value, "tensor", [(i, (i + distance) % tensors) for i in range(tensors)]
        )

    cols = width // CHUNKS_IN
    own, far = [], []
    for c in range(CHUNKS_IN):
        piece = gens[:, :, c * cols : (c + 1) * cols]
        if aligned:
            part = jnp.stack([piece] + [back(piece, d) for d in range(1, tensors)])
        else:
            part = lax.all_gather(piece, "tensor", axis=1, tiled=True)[None]
        own.append(part)
        far.append(across(part, 2))
    near = [across(p, 1) for p in own]
    far_near = [across(p, 1) for p in far]

    hit = (infos[:, :, :2] == me.astype(F32)).astype(F32)
    used = jnp.sum(hit, axis=2)
    token_weight = jnp.sum(hit * infos[:, :, 2:], axis=2)
    order = jnp.arange(tokens)
    earlier = (order[None, :] < order[:, None]).astype(F32)
    place = jnp.sum(used[:, None, :] * earlier[None], axis=2)
    slot = jnp.arange(MOST, dtype=F32)
    match = used[:, None, :] * (place[:, None, :] == slot[None, :, None]).astype(F32)
    tok = jnp.sum(match * jnp.arange(tokens, dtype=F32), axis=2).astype(jnp.int32).reshape(-1)
    valid = jnp.sum(match, axis=2).astype(jnp.int32).reshape(-1)
    slot_weight = jnp.sum(match * token_weight[:, None, :], axis=2).reshape(-1)

    mask = block_mask[0].astype(BF16)
    gate_mask = jnp.repeat(mask[0], BLK, axis=1)
    up_mask = jnp.repeat(mask[1], BLK, axis=1)
    down_mask = jnp.repeat(mask[2].T, BLK, axis=1)
    down, lam = mask_down(down_weight[0], down_mask, query_all)
    masked, pre = (), []
    parts = CHUNKS_IN - 1
    done = lam
    for i in range(parts):
        start, own[i] = lax.optimization_barrier((center_all, own[i], done))[:2]
        *masked, gate_pre, up_pre = mask_in(
            gate_weight[0], up_weight[0], gate_mask, up_mask, start, i, parts, masked
        )
        pre.append((gate_pre, up_pre))
        done = gate_pre
    gate, up = masked
    gate_center = jnp.concatenate([p[0] for p in pre], axis=1)
    up_center = jnp.concatenate([p[1] for p in pre], axis=1)
    gate_center, own[-1] = lax.optimization_barrier((gate_center, own[-1]))
    sigma = 1.0 / (1.0 + jnp.exp(-gate_center))
    act = gate_center * sigma
    slope = sigma * (1.0 + gate_center * (1.0 - sigma)) * up_center
    hidden_center = (act * up_center).astype(BF16)
    out_center = jnp.dot(hidden_center, down, preferred_element_type=F32)
    last = (((1,), (1,)), ((), ()))
    adjoint = lax.dot_general(
        (lam * slope).astype(BF16), gate, last, preferred_element_type=F32
    ) + lax.dot_general((lam * act).astype(BF16), up, last, preferred_element_type=F32)

    pair_out = jnp.stack([out_center, adjoint]) * token_weight.reshape(1, -1, 1)
    pair_out = pair_out.reshape(2, experts, tokens, width)
    lead = own[0].shape[0]
    hidden_gens = gens_in(
        tok, [own, near, far, far_near], gate, up, slope[:, None, :], act[:, None, :]
    )

    pair_out = after(pair_out, hidden_gens)
    pair_sum = pair_out[:, 0]
    for r in range(1, experts):
        pair_sum = pair_sum + across(pair_out[:, r], r)
    if aligned:
        mine = pair_sum
        for d in range(1, tensors):
            pair_sum = pair_sum + back(mine, d)
    else:
        pair_sum = lax.psum(pair_sum, "tensor")

    def add(*terms):
        return sum(t.astype(F32) for t in terms).astype(BF16)

    cols = width // CHUNKS_OUT
    outs, radii = [], []
    crossing, ordered = [], tok
    for c in range(CHUNKS_OUT):
        if c > 1:
            ordered = after(tok, crossing[c - 2][0])
        out = gens_out(
            ordered, valid, slot_weight, hidden_gens, down, c, cols, lead, tokens, experts
        )
        sent = add(out[2], across(out[3], 1))
        crossing.append((sent, add(out[0], across(out[1], 1))))
    for c in range(CHUNKS_OUT):
        sent, kept = crossing[c]
        block = add(kept, across(sent, 2))
        if aligned:
            token_gens = block[0].astype(F32)
            for d in range(1, tensors):
                token_gens = token_gens + back(block[d], tensors - d).astype(F32)
        else:
            block = block.reshape(tokens, tensors, rows_here, cols).transpose(1, 0, 2, 3)
            got = lax.all_to_all(block, "tensor", split_axis=0, concat_axis=0, tiled=True)
            token_gens = jnp.sum(got.astype(F32), axis=0)
        outs.append(token_gens.astype(BF16))
        radii.append(jnp.sum(jnp.abs(token_gens), axis=1))
    radius = jnp.concatenate(radii, axis=1)
    radius_part = radius.astype(BF16)
    if aligned:
        for d in range(1, tensors):
            radius = radius + back(radius_part, d).astype(F32)
    else:
        radius = lax.psum(radius_part, "tensor").astype(F32)
    return (
        pair_sum[0].astype(BF16),
        jnp.concatenate(outs, axis=2),
        radius,
        pair_sum[1],
    )


def solution(mesh):
    placed = (
        P(("groups", "expert"), None),
        P(("groups", "expert"), "tensor", None),
        P(("groups", "expert"), None),
        P(("groups", "expert"), None),
        P(("groups", "expert"), None),
        P("expert", None, "tensor"),
        P("expert", None, "tensor"),
        P("expert", "tensor", None),
        P("expert", None, None, "tensor"),
    )
    return jax.shard_map(
        shards,
        mesh=mesh,
        in_specs=placed,
        out_specs=(
            P(("groups", "expert"), None),
            P(("groups", "expert"), "tensor", None),
            P(("groups", "expert"), None),
            P(("groups", "expert"), None),
        ),
        check_vma=False,
    )
```
